512 devices in a mesh: dp: 32 (over y, x, core), tensor: 16 (over z).
Axes of the slice: x: 4, y: 4, z: 16, core: 2. Of those that a mesh axis runs over, the one named last changes fastest.
Arguments:
- rows_in: bfloat16 [16384, 8192], P('dp', 'tensor'), may hold values from -6 to 6
- adapter_ids: int32 [16384], P('dp'), may hold values from 0 to 511, as said below
- row_counts: int32 [32], P('dp'), may hold values from 256 to 512, as said below
- adapter_slot: int32 [512], replicated, may hold values from 0 to 511, each once
- adapter_a: bfloat16 [512, 16, 16], P(('dp', 'tensor')), may hold values from -1.5 to 1.5
- adapter_b: bfloat16 [512, 512, 1792], P(('dp', 'tensor')), may hold values from -0.25 to 0.25
Outputs:
- delta: bfloat16 [16384, 28672], P('dp', 'tensor')
The draws below stay inside these ranges and needn't reach their ends.
Inputs may be any that keep to these rules, and one draw needn't show every extreme that they name: `adapter_ids`: within the 512 rows of one dp group (live or not), every adapter that is named is named by exactly 2 rows; some adapter is named by 2 live rows in every group. The live rows of a group are its first row_counts rows; some group has all 512 rows live. `adapter_slot`: each storage index appears once; storage index s is held by the device whose flattened dp, tensor index is s.
All inputs are finite; a program needn't handle non-finite values.
Results may differ from the reference program's by a relative error of at most 0.0049.
Values may be sent and summed in bfloat16 or wider, within the bound.
A program may use at most 128 MiB of HBM per device.

```python
import jax
import jax.numpy as jnp
from jax import lax

D = 8192
FF = 28672
FA = 16
ROWS_G = 512
CAP = 2
BIN = 512
BOUT = 1792
ADAPTERS = 512
ROWS = 16384
N_DP = 32


def common_draw(key):
    base = jax.random.fold_in(key, 11)
    keys = jax.random.split(base, 5)
    counts = jax.random.randint(keys[0], (N_DP,), ROWS_G // 2, ROWS_G + 1)
    full_group = jax.random.randint(keys[1], (), 0, N_DP)
    counts = jnp.where(jnp.arange(N_DP) == full_group, ROWS_G, counts).astype(jnp.int32)
    popular = jax.random.permutation(keys[2], ADAPTERS).astype(jnp.int32)
    hottest = jnp.argsort(popular, stable=True)[0]
    noise = jax.random.randint(keys[3], (N_DP, ADAPTERS), 0, 1024)
    score = noise * 64 // (8 + popular[None, :])
    catalog = jnp.arange(ADAPTERS, dtype=jnp.int32)
    score = score * ADAPTERS + catalog[None, :]
    score = jnp.where(catalog[None, :] == hottest, 2 ** 30, score).astype(jnp.int32)
    chosen = lax.top_k(score, ROWS_G // CAP)[1].astype(jnp.int32)
    layout = jnp.repeat(chosen, CAP, axis=1)
    half_rows = ROWS_G // 2
    group_keys = jax.random.split(keys[4], N_DP)
    perm_low = jax.vmap(lambda k: jax.random.permutation(k, half_rows))(group_keys)
    perm_high = jax.vmap(lambda k: jax.random.permutation(jax.random.fold_in(k, 1), ROWS_G - half_rows))(group_keys) + half_rows
    order_rows = jnp.concatenate([perm_low, perm_high], axis=1).astype(jnp.int32)
    picked = jnp.take_along_axis(layout, order_rows, axis=1)
    return (counts, picked.reshape(-1).astype(jnp.int32))


def draw_adapter_ids(key, part):
    return common_draw(key)[1]


def draw_row_counts(key, part):
    return common_draw(key)[0]


def level_of(rng, extent, cuts, low, largest):
    level = 1.0
    for axis_at, shards_of in cuts:
        steps = jax.random.uniform(jax.random.fold_in(jax.random.fold_in(rng, 6), axis_at), (shards_of,), jnp.float32, low / len(cuts), largest / len(cuts))
        level = level * jnp.repeat(jnp.exp(steps), extent[axis_at] // shards_of).reshape((-1,) + (1,) * (len(extent) - 1 - axis_at))
    return level


def scatter_about(stream_key, extent, scale, limit, cuts=(), kind=jnp.bfloat16):
    factor_of = level_of(stream_key, extent, cuts, -0.22, 0.18) if cuts else 1.0
    values = jax.random.normal(stream_key, extent, jnp.float32) * scale * factor_of
    return jnp.minimum(jnp.maximum(values, -limit), limit).astype(kind)


def setup_inputs(seed: int = 0) -> dict:
    arg_keys = jax.random.split(jax.random.key(seed), 7)
    return {
        "rows_in": scatter_about(arg_keys[0], (ROWS, D), 1.0, 6.0, ((0, 32), (1, 16))),
        "adapter_ids": draw_adapter_ids(jax.random.fold_in(arg_keys[6], 71), 0),
        "row_counts": draw_row_counts(jax.random.fold_in(arg_keys[6], 71), 0),
        "adapter_slot": jax.random.permutation(arg_keys[3], ADAPTERS).astype(jnp.int32),
        "adapter_a": scatter_about(arg_keys[4], (ADAPTERS, FA, FA), FA ** -0.5, 1.5, ((0, 512),)),
        "adapter_b": scatter_about(arg_keys[5], (ADAPTERS, BIN, BOUT), BIN ** -0.5, 0.25, ((0, 512),)),
    }


def reference(rows_in, adapter_ids, row_counts, adapter_slot, adapter_a, adapter_b):
    slot = adapter_slot[adapter_ids].astype(jnp.int32)
    position = jnp.arange(ROWS, dtype=jnp.int32)
    row_live = (position % ROWS_G) < row_counts[position // ROWS_G]
    block_size = 16
    block_count = ROWS // block_size

    def one_block(pieces):
        block_rows, block_slot, block_live = pieces
        factor_small = adapter_a[block_slot].astype(jnp.float32)
        factor_large = adapter_b[block_slot].astype(jnp.float32)
        shaped = block_rows.reshape(block_size, FA, BIN).astype(jnp.float32)
        mixed = jnp.einsum("rij,rik->rkj", shaped, factor_small).astype(jnp.bfloat16)
        result = jnp.einsum("rkj,rjl->rkl", mixed.astype(jnp.float32), factor_large)
        result = jnp.where(block_live[:, None, None], result, jnp.float32(0.0))
        return result.reshape(block_size, FF).astype(jnp.bfloat16)

    outputs = lax.map(one_block, (rows_in.reshape(block_count, block_size, D),
                                  slot.reshape(block_count, block_size),
                                  row_live.reshape(block_count, block_size)))
    return outputs.reshape(ROWS, FF)
```

```python
import functools

import jax
import jax.numpy as jnp
from jax import lax
from jax.experimental import pallas as pl
from jax.experimental.pallas import tpu as pltpu
from jax.sharding import PartitionSpec as P

CAP = 2
IN_CHUNK = 128
OUT_CHUNK = 256
ROW_BLOCK = 256
MESH = pl.DeviceIdType.MESH


def one_hot(mask):
    return jnp.where(mask, 1.0, 0.0).astype(jnp.bfloat16)


def dot(left, right):
    return jnp.dot(left, right, preferred_element_type=jnp.float32)


def exchange_kernel(
    n_dp,
    n_t,
    width,
    row_block,
    cs_row_ref,
    kc_row_ref,
    kc_col_ref,
    cs_col_ref,
    x_ref,
    mix_ref,
    b_ref,
    out_ref,
    pack_mat,
    spread_mat,
    gather_mat,
    place_mat,
    in_z_src,
    in_z_dst,
    in_d_src,
    in_d_dst,
    mixed,
    out_d_src,
    out_d_dst,
    out_z_src,
    out_z_dst,
    in_z_send,
    in_z_recv,
    in_d_send,
    in_d_recv,
    out_d_send,
    out_d_recv,
    out_z_send,
    out_z_recv,
):
    g = lax.axis_index("dp")
    t = lax.axis_index("tensor")
    in_chunks, packed, in_cols = in_z_src.shape
    out_chunks, slots, out_cols = out_d_src.shape
    per_group = slots // n_dp
    rows = x_ref.shape[0]

    barrier = pltpu.get_barrier_semaphore()

    def greet_t(step, carry):
        pl.semaphore_signal(
            barrier, inc=1, device_id=(g, lax.rem(t + step, n_t)), device_id_type=MESH
        )
        return carry

    def greet_d(step, carry):
        pl.semaphore_signal(
            barrier, inc=1, device_id=(lax.rem(g + step, n_dp), t), device_id_type=MESH
        )
        return carry

    lax.fori_loop(1, n_t, greet_t, 0)
    lax.fori_loop(1, n_dp, greet_d, 0)

    def blocks(total, body):
        size = min(row_block, total)

        def step(at, carry):
            body(pl.multiple_of(at * size, size), size)
            return carry

        lax.fori_loop(0, total // size, step, 0)

    def z_distance(step):
        half = (step + 1) // 2
        return n_t // 2 + jnp.where(step % 2 == 1, half, -half)

    def send_z(src, dst, chunk, send_sem, recv_sem):
        def step(at, carry):
            peer = lax.rem(t + z_distance(at), n_t)
            pltpu.make_async_remote_copy(
                src_ref=src.at[chunk, pl.ds(pl.multiple_of(peer * width, width), width)],
                dst_ref=dst.at[chunk, pl.ds(pl.multiple_of(t * width, width), width)],
                send_sem=send_sem.at[chunk],
                recv_sem=recv_sem.at[chunk],
                device_id=(g, peer),
                device_id_type=MESH,
            ).start()
            return carry

        lax.fori_loop(0, n_t - 1, step, 0)
        own = pl.ds(pl.multiple_of(t * width, width), width)
        pltpu.make_async_copy(
            src.at[chunk, own], dst.at[chunk, own], recv_sem.at[chunk]
        ).start()

    def send_d(src, dst, chunk, send_sem, recv_sem):
        def step(at, carry):
            peer = lax.rem(g + at, n_dp)
            pltpu.make_async_remote_copy(
                src_ref=src.at[chunk, pl.ds(pl.multiple_of(peer * per_group, per_group), per_group)],
                dst_ref=dst.at[chunk, pl.ds(pl.multiple_of(g * per_group, per_group), per_group)],
                send_sem=send_sem.at[chunk],
                recv_sem=recv_sem.at[chunk],
                device_id=(peer, t),
                device_id_type=MESH,
            ).start()
            return carry

        lax.fori_loop(1, n_dp, step, 0)
        own = pl.ds(pl.multiple_of(g * per_group, per_group), per_group)
        pltpu.make_async_copy(
            src.at[chunk, own], dst.at[chunk, own], recv_sem.at[chunk]
        ).start()

    def arrived(dst, chunk, recv_sem):
        pltpu.make_async_copy(dst.at[chunk], dst.at[chunk], recv_sem.at[chunk]).wait()

    def sent(src, count, chunks, send_sem):
        def step(chunk, carry):
            part = src.at[chunk, pl.ds(0, count)]
            pltpu.make_async_copy(part, part, send_sem.at[chunk]).wait()
            return carry

        lax.fori_loop(0, chunks, step, 0)

    def fill_pack(at, size):
        index = lax.broadcasted_iota(jnp.int32, (size, rows), 0) + at
        pack_mat[pl.ds(at, size), :] = one_hot(index == cs_row_ref[...])

    blocks(packed, fill_pack)

    def pack_chunk(chunk):
        columns = pl.ds(pl.multiple_of(chunk * in_cols, in_cols), in_cols)

        def body(at, size):
            in_z_src[chunk, pl.ds(at, size), :] = dot(
                pack_mat[pl.ds(at, size), :], x_ref[:, columns]
            ).astype(jnp.bfloat16)

        blocks(packed, body)

    pack_chunk(0)
    pl.semaphore_wait(barrier, n_dp + n_t - 2)

    def start_in(chunk, carry):
        send_z(in_z_src, in_z_dst, chunk, in_z_send, in_z_recv)

        @pl.when(chunk < in_chunks - 1)
        def _():
            pack_chunk(chunk + 1)

        return carry

    lax.fori_loop(0, in_chunks, start_in, 0)

    def fill_spread(at, size):
        index = lax.broadcasted_iota(jnp.int32, (size, packed), 0) + at
        spread_mat[pl.ds(at, size), :] = one_hot(index == kc_row_ref[...])

    def fill_gather(at, size):
        index = lax.broadcasted_iota(jnp.int32, (size, slots), 1)
        gather_mat[pl.ds(at, size), :] = one_hot(index == kc_col_ref[pl.ds(at, size), :])

    def fill_place(at, size):
        index = lax.broadcasted_iota(jnp.int32, (size, packed), 1)
        place_mat[pl.ds(at, size), :] = one_hot(index == cs_col_ref[pl.ds(at, size), :])

    blocks(slots, fill_spread)
    blocks(packed, fill_gather)
    blocks(rows, fill_place)

    def spread_chunk(chunk, carry):
        arrived(in_z_dst, chunk, in_z_recv)

        def body(at, size):
            in_d_src[chunk, pl.ds(at, size), :] = dot(
                spread_mat[pl.ds(at, size), :], in_z_dst[chunk]
            ).astype(jnp.bfloat16)

        blocks(slots, body)
        send_d(in_d_src, in_d_dst, chunk, in_d_send, in_d_recv)
        return carry

    lax.fori_loop(0, in_chunks, spread_chunk, 0)

    for chunk in range(in_chunks):
        arrived(in_d_dst, chunk, in_d_recv)

        def mix(at, size):
            mixed[pl.ds(at, size), chunk * in_cols : (chunk + 1) * in_cols] = dot(
                mix_ref[...], in_d_dst[chunk, pl.ds(at, size), :]
            ).astype(jnp.bfloat16)

        blocks(slots, mix)

    def start_out(chunk):
        columns = pl.ds(pl.multiple_of(chunk * out_cols, out_cols), out_cols)

        def body(at, size):
            out_d_src[chunk, pl.ds(at, size), :] = dot(
                mixed[pl.ds(at, size), :], b_ref[:, columns]
            ).astype(jnp.bfloat16)

        blocks(slots, body)
        send_d(out_d_src, out_d_dst, chunk, out_d_send, out_d_recv)

    start_out(0)
    start_out(1)

    def relay(chunk, carry):
        arrived(out_d_dst, chunk, out_d_recv)

        def body(at, size):
            out_z_src[chunk, pl.ds(at, size), :] = dot(
                gather_mat[pl.ds(at, size), :], out_d_dst[chunk]
            ).astype(jnp.bfloat16)

        blocks(packed, body)
        send_z(out_z_src, out_z_dst, chunk, out_z_send, out_z_recv)

        @pl.when(chunk + 2 < out_chunks)
        def _():
            start_out(chunk + 2)

        return carry

    lax.fori_loop(0, out_chunks, relay, 0)

    def place(chunk, carry):
        arrived(out_z_dst, chunk, out_z_recv)
        columns = pl.ds(pl.multiple_of(chunk * out_cols, out_cols), out_cols)

        def body(at, size):
            out_ref[pl.ds(at, size), columns] = dot(
                place_mat[pl.ds(at, size), :], out_z_dst[chunk]
            ).astype(jnp.bfloat16)

        blocks(rows, body)
        return carry

    lax.fori_loop(0, out_chunks, place, 0)

    sent(in_z_src, (n_t - 1) * width, in_chunks, in_z_send)
    sent(in_d_src, (n_dp - 1) * per_group, in_chunks, in_d_send)
    sent(out_d_src, (n_dp - 1) * per_group, out_chunks, out_d_send)
    sent(out_z_src, (n_t - 1) * width, out_chunks, out_z_send)


def on_device(rows_in, adapter_ids, row_counts, adapter_slot, adapter_a, adapter_b):
    n_dp = lax.axis_size("dp")
    n_t = lax.axis_size("tensor")
    rows, in_width = rows_in.shape
    order = adapter_a.shape[1]
    out_width = adapter_b.shape[2]
    width = n_dp * CAP
    packed = n_t * width
    per_group = order * CAP
    slots = n_dp * per_group
    row_block = min(ROW_BLOCK, slots)

    catalog = jnp.arange(adapter_slot.shape[0], dtype=jnp.int32)
    owner = jnp.sum(
        jnp.where(adapter_ids[:, None] == catalog[None, :], adapter_slot[None, :], 0), axis=1
    )
    position = jnp.arange(rows, dtype=jnp.int32)
    live = position < row_counts[0]
    earlier = position[None, :] < position[:, None]
    rank = jnp.sum(
        ((adapter_ids[:, None] == adapter_ids[None, :]) & earlier).astype(jnp.int32), axis=1
    )
    column = owner % n_t
    place = jnp.sum(
        ((column[:, None] == column[None, :]) & earlier & live[None, :]).astype(jnp.int32), axis=1
    )
    packed_at = jnp.where(live, column * width + place, -1)
    slot_at = (owner // n_t) * per_group + rank
    mine = lax.axis_index("tensor") * width + jnp.arange(width, dtype=jnp.int32)
    key = (
        jnp.sum(jnp.where(packed_at[:, None] == mine[None, :], slot_at[:, None] + 1, 0), axis=0) - 1
    )
    step = jnp.arange(order, dtype=jnp.int32) * CAP
    keys = jnp.where(key[None, :] >= 0, key[None, :] + step[:, None], -1).reshape(packed)

    at = jnp.arange(row_block, dtype=jnp.int32)
    unit = (at // CAP) % order
    pick = (unit[:, None] == jnp.arange(order, dtype=jnp.int32)[None, :]).astype(jnp.bfloat16)
    wide = jnp.dot(jnp.dot(pick, adapter_a[0].T), pick.T)
    same = (at[:, None] // per_group == at[None, :] // per_group) & (
        at[:, None] % CAP == at[None, :] % CAP
    )
    mix = jnp.where(same, wide, jnp.zeros_like(wide))

    in_chunks = max(1, in_width // IN_CHUNK)
    in_cols = in_width // in_chunks
    out_chunks = max(2, out_width // OUT_CHUNK)
    out_cols = out_width // out_chunks
    dma = pltpu.SemaphoreType.DMA
    bf16 = jnp.bfloat16
    return pl.pallas_call(
        functools.partial(exchange_kernel, n_dp, n_t, width, row_block),
        out_shape=jax.ShapeDtypeStruct((rows, out_width), bf16),
        in_specs=[pl.BlockSpec(memory_space=pltpu.VMEM)] * 7,
        out_specs=pl.BlockSpec(memory_space=pltpu.VMEM),
        scratch_shapes=[
            pltpu.VMEM((packed, rows), bf16),
            pltpu.VMEM((slots, packed), bf16),
            pltpu.VMEM((packed, slots), bf16),
            pltpu.VMEM((rows, packed), bf16),
            pltpu.VMEM((in_chunks, packed, in_cols), bf16),
            pltpu.VMEM((in_chunks, packed, in_cols), bf16),
            pltpu.VMEM((in_chunks, slots, in_cols), bf16),
            pltpu.VMEM((in_chunks, slots, in_cols), bf16),
            pltpu.VMEM((slots, in_width), bf16),
            pltpu.VMEM((out_chunks, slots, out_cols), bf16),
            pltpu.VMEM((out_chunks, slots, out_cols), bf16),
            pltpu.VMEM((out_chunks, packed, out_cols), bf16),
            pltpu.VMEM((out_chunks, packed, out_cols), bf16),
            dma((in_chunks,)),
            dma((in_chunks,)),
            dma((in_chunks,)),
            dma((in_chunks,)),
            dma((out_chunks,)),
            dma((out_chunks,)),
            dma((out_chunks,)),
            dma((out_chunks,)),
        ],
        compiler_params=pltpu.CompilerParams(
            collective_id=0, has_side_effects=True, vmem_limit_bytes=56 * 1024 * 1024
        ),
        cost_estimate=pl.CostEstimate(
            flops=2 * slots * in_width * out_width, bytes_accessed=10_000_000, transcendentals=0
        ),
    )(
        packed_at[None, :],
        keys[None, :],
        keys[:, None],
        packed_at[:, None],
        rows_in,
        mix,
        adapter_b[0],
    )


def solution(mesh):
    return jax.shard_map(
        on_device,
        mesh=mesh,
        in_specs=(
            P("dp", "tensor"),
            P("dp"),
            P("dp"),
            P(),
            P(("dp", "tensor"), None, None),
            P(("dp", "tensor"), None, None),
        ),
        out_specs=P("dp", "tensor"),
        check_vma=False,
    )
```

```python
import functools

import jax
import jax.numpy as jnp
from jax import lax
from jax.experimental import pallas as pl
from jax.experimental.pallas import tpu as pltpu
from jax.sharding import PartitionSpec as P

CAP = 2
IN_CHUNK = 128
OUT_CHUNK = 256
ROW_BLOCK = 256
MESH = pl.DeviceIdType.MESH


def one_hot(mask):
    return jnp.where(mask, 1.0, 0.0).astype(jnp.bfloat16)


def dot(left, right):
    return jnp.dot(left, right, preferred_element_type=jnp.float32)


def plan_kernel(
    n_dp, n_t, per_group, ids_ref, slot_ref, count_ref, rows_ref, cols_ref, most_ref,
    mine, peers, send_sem, recv_sem
):
    g = lax.axis_index("dp")
    t = lax.axis_index("tensor")
    rows = ids_ref.shape[1]
    tile = mine.shape[0]
    barrier = pltpu.get_barrier_semaphore()

    def greet(step, carry):
        pl.semaphore_signal(
            barrier, inc=1, device_id=(lax.rem(g + step, n_dp), t), device_id_type=MESH
        )
        return carry

    lax.fori_loop(1, n_dp, greet, 0)
    down = lax.broadcasted_iota(jnp.int32, (rows, rows), 0)
    across = lax.broadcasted_iota(jnp.int32, (rows, rows), 1)

    def turned(row):
        return jnp.sum(jnp.where(down == across, row, 0), axis=1, keepdims=True)

    def counted(mask, axis):
        return jnp.sum(jnp.where(mask, 1, 0), axis=axis, keepdims=True)

    ids = ids_ref[...]
    ids_col = turned(ids)
    owner_col = jnp.sum(jnp.where(ids_col == across, slot_ref[...], 0), axis=1, keepdims=True)
    owner = jnp.sum(jnp.where(down == across, owner_col, 0), axis=0, keepdims=True)
    live = across < count_ref[...]
    live_col = down < count_ref[...]
    column = lax.rem(owner, n_t)
    column_col = lax.rem(owner_col, n_t)
    alike = column_col == column
    place = counted(alike & (down < across) & live_col, 0)
    lane = lax.broadcasted_iota(jnp.int32, (1, rows), 1)
    is_live = lane < count_ref[...]
    width = CAP * n_dp
    code = jnp.where(is_live, column * width + place, -1)
    most = jnp.max(jnp.where(is_live, place + 1, 0), axis=1, keepdims=True)
    mine[...] = jnp.broadcast_to(most.astype(jnp.float32), mine.shape)

    pl.semaphore_wait(barrier, n_dp - 1)

    def send(step, carry):
        peer = lax.rem(g + step, n_dp)
        pltpu.make_async_remote_copy(
            src_ref=mine,
            dst_ref=peers.at[pl.ds(pl.multiple_of(g * tile, tile), tile)],
            send_sem=send_sem,
            recv_sem=recv_sem,
            device_id=(peer, t),
            device_id_type=MESH,
        ).start()
        return carry

    lax.fori_loop(1, n_dp, send, 0)
    pltpu.make_async_copy(
        mine, peers.at[pl.ds(pl.multiple_of(g * tile, tile), tile)], recv_sem
    ).start()

    same = ids_col == ids
    slot_at = lax.div(owner, n_t) * per_group + counted(same & (down < across), 0)
    rows_ref[0:1, :] = code
    rows_ref[1:2, :] = slot_at
    place_col = counted(alike & (across < down) & live, 1)
    index = lax.broadcasted_iota(jnp.int32, (rows, 1), 0)
    code_col = jnp.where(index < count_ref[...], column_col * width + place_col, -1)
    slot_col = lax.div(owner_col, n_t) * per_group + counted(same & (across < down), 1)
    side = lax.broadcasted_iota(jnp.int32, cols_ref.shape, 1)
    cols_ref[...] = jnp.where(side == 0, code_col, slot_col)

    pltpu.make_async_copy(peers, peers, recv_sem).wait()
    most_ref[...] = jnp.max(peers[...], axis=0, keepdims=True).astype(jnp.int32)
    part = peers.at[pl.ds(0, (n_dp - 1) * tile)]
    pltpu.make_async_copy(part, part, send_sem).wait()


def exchange_kernel(
    n_dp,
    n_t,
    width,
    row_block,
    rows_ref,
    cols_ref,
    x_ref,
    a_ref,
    b_ref,
    out_ref,
    mix_mat,
    pack_mat,
    spread_mat,
    gather_mat,
    place_mat,
    in_z_src,
    in_z_dst,
    in_d_src,
    in_d_dst,
    mixed,
    out_d_src,
    out_d_dst,
    out_z_src,
    out_z_dst,
    in_z_send,
    in_z_recv,
    in_d_send,
    in_d_recv,
    out_d_send,
    out_d_recv,
    out_z_send,
    out_z_recv,
):
    g = lax.axis_index("dp")
    t = lax.axis_index("tensor")
    in_chunks, packed, in_cols = in_z_src.shape
    out_chunks, slots, out_cols = out_d_src.shape
    per_group = slots // n_dp
    rows = x_ref.shape[0]

    barrier = pltpu.get_barrier_semaphore()

    def greet_t(step, carry):
        pl.semaphore_signal(
            barrier, inc=1, device_id=(g, lax.rem(t + step, n_t)), device_id_type=MESH
        )
        return carry

    def greet_d(step, carry):
        pl.semaphore_signal(
            barrier, inc=1, device_id=(lax.rem(g + step, n_dp), t), device_id_type=MESH
        )
        return carry

    lax.fori_loop(1, n_t, greet_t, 0)
    lax.fori_loop(1, n_dp, greet_d, 0)

    def blocks(total, body):
        size = min(row_block, total)

        def step(at, carry):
            body(pl.multiple_of(at * size, size), size)
            return carry

        lax.fori_loop(0, total // size, step, 0)

    def z_distance(step):
        half = (step + 1) // 2
        return n_t // 2 + jnp.where(step % 2 == 1, half, -half)

    def send_z(src, dst, chunk, send_sem, recv_sem):
        def step(at, carry):
            peer = lax.rem(t + z_distance(at), n_t)
            pltpu.make_async_remote_copy(
                src_ref=src.at[chunk, pl.ds(pl.multiple_of(peer * width, width), width)],
                dst_ref=dst.at[chunk, pl.ds(pl.multiple_of(t * width, width), width)],
                send_sem=send_sem.at[chunk],
                recv_sem=recv_sem.at[chunk],
                device_id=(g, peer),
                device_id_type=MESH,
            ).start()
            return carry

        lax.fori_loop(0, n_t - 1, step, 0)
        own = pl.ds(pl.multiple_of(t * width, width), width)
        pltpu.make_async_copy(
            src.at[chunk, own], dst.at[chunk, own], recv_sem.at[chunk]
        ).start()

    def send_d(src, dst, chunk, send_sem, recv_sem):
        def step(at, carry):
            peer = lax.rem(g + at, n_dp)
            pltpu.make_async_remote_copy(
                src_ref=src.at[chunk, pl.ds(pl.multiple_of(peer * per_group, per_group), per_group)],
                dst_ref=dst.at[chunk, pl.ds(pl.multiple_of(g * per_group, per_group), per_group)],
                send_sem=send_sem.at[chunk],
                recv_sem=recv_sem.at[chunk],
                device_id=(peer, t),
                device_id_type=MESH,
            ).start()
            return carry

        lax.fori_loop(1, n_dp, step, 0)
        own = pl.ds(pl.multiple_of(g * per_group, per_group), per_group)
        pltpu.make_async_copy(
            src.at[chunk, own], dst.at[chunk, own], recv_sem.at[chunk]
        ).start()

    def arrived(dst, chunk, recv_sem):
        pltpu.make_async_copy(dst.at[chunk], dst.at[chunk], recv_sem.at[chunk]).wait()

    def sent(src, count, chunks, send_sem):
        def step(chunk, carry):
            part = src.at[chunk, pl.ds(0, count)]
            pltpu.make_async_copy(part, part, send_sem.at[chunk]).wait()
            return carry

        lax.fori_loop(0, chunks, step, 0)

    full = CAP * n_dp

    def repack(code):
        return jnp.where(code >= 0, lax.div(code, full) * width + lax.rem(code, full), -1)

    code = rows_ref[0:1, :]
    code_col = cols_ref[:, 0:1]
    packed_at = repack(code)
    packed_at_col = repack(code_col)

    def fill_pack(at, size):
        index = lax.broadcasted_iota(jnp.int32, (size, rows), 0) + at
        pack_mat[pl.ds(at, size), :] = one_hot(index == packed_at)

    blocks(packed, fill_pack)

    def pack_chunk(chunk):
        columns = pl.ds(pl.multiple_of(chunk * in_cols, in_cols), in_cols)

        def body(at, size):
            in_z_src[chunk, pl.ds(at, size), :] = dot(
                pack_mat[pl.ds(at, size), :], x_ref[:, columns]
            ).astype(jnp.bfloat16)

        blocks(packed, body)

    pack_chunk(0)
    pl.semaphore_wait(barrier, n_dp + n_t - 2)

    def start_in(chunk, carry):
        send_z(in_z_src, in_z_dst, chunk, in_z_send, in_z_recv)

        @pl.when(chunk < in_chunks - 1)
        def _():
            pack_chunk(chunk + 1)

        return carry

    lax.fori_loop(0, in_chunks, start_in, 0)

    order = a_ref.shape[0]
    first = t * width
    spot = lax.broadcasted_iota(jnp.int32, (1, packed), 1)
    key = jnp.sum(
        jnp.where(packed_at_col == first + lax.rem(spot, width), cols_ref[:, 1:2] + 1, 0),
        axis=0,
        keepdims=True,
    )
    key = jnp.where(key > 0, key - 1 + lax.div(spot, width) * CAP, -1)

    def fill_spread(at, size):
        index = lax.broadcasted_iota(jnp.int32, (size, packed), 0) + at
        spread_mat[pl.ds(at, size), :] = one_hot(index == key)

    def fill_gather(at, size):
        spot = lax.broadcasted_iota(jnp.int32, (size, 1), 0) + at
        key = jnp.sum(
            jnp.where(packed_at == first + lax.rem(spot, width), rows_ref[1:2, :] + 1, 0),
            axis=1,
            keepdims=True,
        )
        key = jnp.where(key > 0, key - 1 + lax.div(spot, width) * CAP, -1)
        index = lax.broadcasted_iota(jnp.int32, (size, slots), 1)
        gather_mat[pl.ds(at, size), :] = one_hot(index == key)

    def fill_place(at, size):
        index = lax.broadcasted_iota(jnp.int32, (size, packed), 1)
        target = repack(cols_ref[pl.ds(at, size), 0:1])
        place_mat[pl.ds(at, size), :] = one_hot(index == target)

    side = mix_mat.shape[0]
    unit = lax.rem(lax.div(lax.broadcasted_iota(jnp.int32, (side, order), 0), CAP), order)
    pick = one_hot(unit == lax.broadcasted_iota(jnp.int32, (side, order), 1))
    contract = (((1,), (1,)), ((), ()))
    tall = lax.dot_general(pick, a_ref[...], contract, preferred_element_type=jnp.float32)
    wide = lax.dot_general(
        tall.astype(jnp.bfloat16), pick, contract, preferred_element_type=jnp.float32
    )
    down = lax.broadcasted_iota(jnp.int32, (side, side), 0)
    across = lax.broadcasted_iota(jnp.int32, (side, side), 1)
    same = (lax.div(down, per_group) == lax.div(across, per_group)) & (
        lax.rem(down, CAP) == lax.rem(across, CAP)
    )
    mix_mat[...] = jnp.where(same, wide, 0.0).astype(jnp.bfloat16)

    blocks(slots, fill_spread)
    blocks(packed, fill_gather)
    blocks(rows, fill_place)

    def spread_chunk(chunk, carry):
        arrived(in_z_dst, chunk, in_z_recv)

        def body(at, size):
            in_d_src[chunk, pl.ds(at, size), :] = dot(
                spread_mat[pl.ds(at, size), :], in_z_dst[chunk]
            ).astype(jnp.bfloat16)

        blocks(slots, body)
        send_d(in_d_src, in_d_dst, chunk, in_d_send, in_d_recv)
        return carry

    lax.fori_loop(0, in_chunks, spread_chunk, 0)

    for chunk in range(in_chunks):
        arrived(in_d_dst, chunk, in_d_recv)

        def mix(at, size):
            mixed[pl.ds(at, size), chunk * in_cols : (chunk + 1) * in_cols] = dot(
                mix_mat[...], in_d_dst[chunk, pl.ds(at, size), :]
            ).astype(jnp.bfloat16)

        blocks(slots, mix)

    def start_out(chunk):
        columns = pl.ds(pl.multiple_of(chunk * out_cols, out_cols), out_cols)

        def body(at, size):
            out_d_src[chunk, pl.ds(at, size), :] = dot(
                mixed[pl.ds(at, size), :], b_ref[:, columns]
            ).astype(jnp.bfloat16)

        blocks(slots, body)
        send_d(out_d_src, out_d_dst, chunk, out_d_send, out_d_recv)

    start_out(0)
    start_out(1)

    def relay(chunk, carry):
        arrived(out_d_dst, chunk, out_d_recv)

        def body(at, size):
            out_z_src[chunk, pl.ds(at, size), :] = dot(
                gather_mat[pl.ds(at, size), :], out_d_dst[chunk]
            ).astype(jnp.bfloat16)

        blocks(packed, body)
        send_z(out_z_src, out_z_dst, chunk, out_z_send, out_z_recv)

        @pl.when(chunk + 2 < out_chunks)
        def _():
            start_out(chunk + 2)

        return carry

    lax.fori_loop(0, out_chunks, relay, 0)

    def place(chunk, carry):
        arrived(out_z_dst, chunk, out_z_recv)
        columns = pl.ds(pl.multiple_of(chunk * out_cols, out_cols), out_cols)

        def body(at, size):
            out_ref[pl.ds(at, size), columns] = dot(
                place_mat[pl.ds(at, size), :], out_z_dst[chunk]
            ).astype(jnp.bfloat16)

        blocks(rows, body)
        return carry

    lax.fori_loop(0, out_chunks, place, 0)

    sent(in_z_src, (n_t - 1) * width, in_chunks, in_z_send)
    sent(in_d_src, (n_dp - 1) * per_group, in_chunks, in_d_send)
    sent(out_d_src, (n_dp - 1) * per_group, out_chunks, out_d_send)
    sent(out_z_src, (n_t - 1) * width, out_chunks, out_z_send)


def exchange(width, collective_id, row_plan, col_plan, rows_in, small, large):
    n_dp = lax.axis_size("dp")
    n_t = lax.axis_size("tensor")
    rows, in_width = rows_in.shape
    order = small.shape[0]
    out_width = large.shape[1]
    packed = n_t * width
    slots = n_dp * order * CAP
    row_block = min(ROW_BLOCK, slots)
    in_chunks = max(1, in_width // IN_CHUNK)
    in_cols = in_width // in_chunks
    out_chunks = max(2, out_width // OUT_CHUNK)
    out_cols = out_width // out_chunks
    dma = pltpu.SemaphoreType.DMA
    bf16 = jnp.bfloat16
    return pl.pallas_call(
        functools.partial(exchange_kernel, n_dp, n_t, width, row_block),
        out_shape=jax.ShapeDtypeStruct((rows, out_width), bf16),
        in_specs=[pl.BlockSpec(memory_space=pltpu.VMEM)] * 5,
        out_specs=pl.BlockSpec(memory_space=pltpu.VMEM),
        scratch_shapes=[
            pltpu.VMEM((row_block, row_block), bf16),
            pltpu.VMEM((packed, rows), bf16),
            pltpu.VMEM((slots, packed), bf16),
            pltpu.VMEM((packed, slots), bf16),
            pltpu.VMEM((rows, packed), bf16),
            pltpu.VMEM((in_chunks, packed, in_cols), bf16),
            pltpu.VMEM((in_chunks, packed, in_cols), bf16),
            pltpu.VMEM((in_chunks, slots, in_cols), bf16),
            pltpu.VMEM((in_chunks, slots, in_cols), bf16),
            pltpu.VMEM((slots, in_width), bf16),
            pltpu.VMEM((out_chunks, slots, out_cols), bf16),
            pltpu.VMEM((out_chunks, slots, out_cols), bf16),
            pltpu.VMEM((out_chunks, packed, out_cols), bf16),
            pltpu.VMEM((out_chunks, packed, out_cols), bf16),
            dma((in_chunks,)),
            dma((in_chunks,)),
            dma((in_chunks,)),
            dma((in_chunks,)),
            dma((out_chunks,)),
            dma((out_chunks,)),
            dma((out_chunks,)),
            dma((out_chunks,)),
        ],
        compiler_params=pltpu.CompilerParams(
            collective_id=collective_id,
            has_side_effects=True,
            vmem_limit_bytes=56 * 1024 * 1024,
        ),
        cost_estimate=pl.CostEstimate(
            flops=2 * slots * in_width * out_width, bytes_accessed=10_000_000, transcendentals=0
        ),
    )(row_plan, col_plan, rows_in, small, large)


def on_device(rows_in, adapter_ids, row_counts, adapter_slot, adapter_a, adapter_b):
    n_dp = lax.axis_size("dp")
    n_t = lax.axis_size("tensor")
    rows = rows_in.shape[0]
    order = adapter_a.shape[1]
    i32 = jnp.int32
    row_plan, col_plan, most = pl.pallas_call(
        functools.partial(plan_kernel, n_dp, n_t, order * CAP),
        out_shape=(
            jax.ShapeDtypeStruct((2, rows), i32),
            jax.ShapeDtypeStruct((rows, 2), i32),
            jax.ShapeDtypeStruct((1, 128), i32),
        ),
        in_specs=[pl.BlockSpec(memory_space=pltpu.VMEM)] * 3,
        out_specs=[pl.BlockSpec(memory_space=pltpu.VMEM)] * 3,
        scratch_shapes=[
            pltpu.VMEM((8, 128), jnp.float32),
            pltpu.VMEM((8 * n_dp, 128), jnp.float32),
            pltpu.SemaphoreType.DMA,
            pltpu.SemaphoreType.DMA,
        ],
        compiler_params=pltpu.CompilerParams(
            collective_id=0, has_side_effects=True, vmem_limit_bytes=32 * 1024 * 1024
        ),
    )(adapter_ids[None, :], adapter_slot[None, :], row_counts[None, :])
    full = CAP * n_dp
    tight = full * 3 // 4
    return lax.cond(
        most[0, 0] <= tight,
        functools.partial(exchange, tight, 1),
        functools.partial(exchange, full, 2),
        row_plan,
        col_plan,
        rows_in,
        adapter_a[0],
        adapter_b[0],
    )


def solution(mesh):
    return jax.shard_map(
        on_device,
        mesh=mesh,
        in_specs=(
            P("dp", "tensor"),
            P("dp"),
            P("dp"),
            P(),
            P(("dp", "tensor"), None, None),
            P(("dp", "tensor"), None, None),
        ),
        out_specs=P("dp", "tensor"),
        check_vma=False,
    )
```

```python
import functools

import jax
import jax.numpy as jnp
from jax import lax
from jax.experimental import pallas as pl
from jax.experimental.pallas import tpu as pltpu
from jax.sharding import PartitionSpec as P

RANKS = 2
IN_CHUNK = 128
OUT_CHUNK = 256
SIDE = 256
MESH = pl.DeviceIdType.MESH
BF16 = jnp.bfloat16
I32 = jnp.int32


def one_hot(mask):
    return jnp.where(mask, 1.0, 0.0).astype(BF16)


def dot(left, right):
    return jnp.dot(left, right, preferred_element_type=jnp.float32)


def iota(shape, axis):
    return lax.broadcasted_iota(I32, shape, axis)


def total(parts):
    return functools.reduce(lambda a, b: a + b, parts)


class Plan:
    def __init__(self, n_dp, rest):
        full = n_dp * RANKS
        self.tight = full * 3 // 4
        self.rest = rest
        if rest:
            self.width = full - self.tight
            self.ranks = (1,)
            self.in_stages = ((0, self.width),)
            self.out_stages = ((0, self.width),)
            self.sources = {1: (0,)}
            self.needs = ((1,),)
        else:
            self.width = self.tight
            self.ranks = (0, 1)
            self.in_stages = ((0, n_dp), (n_dp, self.width))
            self.out_stages = ((0, self.width - n_dp), (self.width - n_dp, self.width))
            self.sources = {0: (0,), 1: (0, 1)}
            self.needs = ((0,), (0, 1))


def exchange_kernel(n_dp, n_t, plan, ids_ref, slot_ref, count_ref, x_ref, a_ref, b_ref, *refs):
    if plan.rest:
        out_ref, mix_mat, ins, mids, outs = refs
        flag = None
    else:
        out_ref, over_ref, mix_mat, ins, mids, outs, flag = refs
    g = lax.axis_index("dp")
    t = lax.axis_index("tensor")
    rows = x_ref.shape[0]
    order = a_ref.shape[0]
    lines = n_dp * order
    width = plan.width
    in_chunks, _, in_cols = ins[0]["src"].shape
    out_chunks, _, out_cols = outs[0]["src"].shape

    barrier = pltpu.get_barrier_semaphore()

    def greet_t(step, carry):
        pl.semaphore_signal(
            barrier, inc=1, device_id=(g, lax.rem(t + step, n_t)), device_id_type=MESH
        )
        return carry

    def greet_d(step, carry):
        pl.semaphore_signal(
            barrier, inc=1, device_id=(lax.rem(g + step, n_dp), t), device_id_type=MESH
        )
        return carry

    lax.fori_loop(1, n_t, greet_t, 0)
    lax.fori_loop(1, n_dp, greet_d, 0)

    def send_z(part, chunk, height):
        src, dst, send_sem, recv_sem = part["src"], part["dst"], part["send"], part["recv"]

        def step(at, carry):
            half = (at + 1) // 2
            distance = n_t // 2 + jnp.where(at % 2 == 1, half, -half)
            peer = lax.rem(t + distance, n_t)
            pltpu.make_async_remote_copy(
                src_ref=src.at[chunk, pl.ds(pl.multiple_of(peer * height, height), height)],
                dst_ref=dst.at[chunk, pl.ds(pl.multiple_of(t * height, height), height)],
                send_sem=send_sem.at[chunk],
                recv_sem=recv_sem.at[chunk],
                device_id=(g, peer),
                device_id_type=MESH,
            ).start()
            return carry

        lax.fori_loop(0, n_t - 1, step, 0)
        own = pl.ds(pl.multiple_of(t * height, height), height)
        pltpu.make_async_copy(
            src.at[chunk, own], dst.at[chunk, own], recv_sem.at[chunk]
        ).start()

    def send_d(src, dst, chunk, send_sem, recv_sem):
        def step(at, carry):
            peer = lax.rem(g + at, n_dp)
            pltpu.make_async_remote_copy(
                src_ref=src.at[chunk, pl.ds(pl.multiple_of(peer * order, order), order)],
                dst_ref=dst.at[chunk, pl.ds(pl.multiple_of(g * order, order), order)],
                send_sem=send_sem.at[chunk],
                recv_sem=recv_sem.at[chunk],
                device_id=(peer, t),
                device_id_type=MESH,
            ).start()
            return carry

        lax.fori_loop(1, n_dp, step, 0)
        own = pl.ds(pl.multiple_of(g * order, order), order)
        pltpu.make_async_copy(
            src.at[chunk, own], dst.at[chunk, own], recv_sem.at[chunk]
        ).start()

    def arrived(dst, chunk, recv_sem):
        pltpu.make_async_copy(dst.at[chunk], dst.at[chunk], recv_sem.at[chunk]).wait()

    def sent(src, height, send_sem):
        chunks, tall, _ = src.shape

        def step(chunk, carry):
            part = src.at[chunk, pl.ds(0, tall - height)]
            pltpu.make_async_copy(part, part, send_sem.at[chunk]).wait()
            return carry

        lax.fori_loop(0, chunks, step, 0)

    def in_columns(chunk):
        return pl.ds(pl.multiple_of(chunk * in_cols, in_cols), in_cols)

    def out_columns(chunk):
        return pl.ds(pl.multiple_of(chunk * out_cols, out_cols), out_cols)

    down = iota((rows, rows), 0)
    across = iota((rows, rows), 1)
    diagonal = down == across
    before = down < across

    def to_column(row):
        return jnp.sum(jnp.where(diagonal, row, 0), axis=1, keepdims=True)

    def to_row(column):
        return jnp.sum(jnp.where(diagonal, column, 0), axis=0, keepdims=True)

    def count(mask):
        return jnp.sum(jnp.where(mask, 1, 0), axis=0, keepdims=True)

    ids = ids_ref[...]
    ids_col = to_column(ids)
    owner_col = jnp.sum(jnp.where(ids_col == across, slot_ref[...], 0), axis=1, keepdims=True)
    rank = count((ids_col == ids) & before)
    owner = to_row(owner_col)
    column = lax.rem(owner, n_t)
    team = column * RANKS + rank
    team_col = to_column(team)
    live = iota((1, rows), 1) < count_ref[...]
    earlier = count((team_col == team) & before)
    firsts = count((team_col == column * RANKS) & (down < count_ref[...]))
    top = plan.tight - 1 - earlier
    over = live & (rank == 1) & (top < firsts)
    if plan.rest:
        code = jnp.where(over, column * width + firsts - 1 - top, -1)
    else:
        place = jnp.where(rank == 1, top, earlier)
        code = jnp.where(live & ~over, column * width + place, -1)

    def pack(stage, chunk):
        ins[stage]["src"][chunk] = dot(ins[stage]["pack"][...], x_ref[:, in_columns(chunk)]).astype(
            BF16
        )

    for stage, (lo, hi) in enumerate(plan.in_stages):
        height = hi - lo
        spot = iota((n_t * height, 1), 0)
        spot = lax.div(spot, height) * width + lo + lax.rem(spot, height)
        ins[stage]["pack"][...] = one_hot(spot == code)
        if stage == 0:
            pack(0, 0)
            pl.semaphore_wait(barrier, n_dp + n_t - 2)

        def start_in(chunk, carry, stage=stage, height=height):
            if stage > 0:
                pack(stage, chunk)
            send_z(ins[stage], chunk, height)
            if stage == 0:

                @pl.when(chunk < in_chunks - 1)
                def _():
                    pack(0, chunk + 1)

            return carry

        lax.fori_loop(0, in_chunks, start_in, 0)

    if flag is not None:
        tile = flag["src"].shape[0]
        most = jnp.max(jnp.where(over, 1.0, 0.0), axis=1, keepdims=True)
        flag["src"][...] = jnp.broadcast_to(most, flag["src"].shape)
        spot = pl.ds(pl.multiple_of(g * tile, tile), tile)

        def tell(step, carry):
            pltpu.make_async_remote_copy(
                src_ref=flag["src"],
                dst_ref=flag["dst"].at[spot],
                send_sem=flag["send"],
                recv_sem=flag["recv"],
                device_id=(lax.rem(g + step, n_dp), t),
                device_id_type=MESH,
            ).start()
            return carry

        lax.fori_loop(1, n_dp, tell, 0)
        pltpu.make_async_copy(flag["src"], flag["dst"].at[spot], flag["recv"]).start()

    code_col = to_column(code)
    rank_col = lax.rem(team_col, RANKS)
    line = lax.div(owner, n_t) * order + 1
    line_col = lax.div(owner_col, n_t) * order + 1
    first = t * width

    def build_spread(half):
        mid = mids[plan.ranks.index(half)]
        for at, stage in enumerate(plan.sources[half]):
            lo, hi = plan.in_stages[stage]
            height = hi - lo
            lane = iota((1, n_t * height), 1)
            here = (code_col == first + lo + lax.rem(lane, height)) & (rank_col == half)
            key = jnp.sum(jnp.where(here, line_col, 0), axis=0, keepdims=True)
            key = jnp.where(key > 0, key - 1 + lax.div(lane, height), -1)
            mid["spread"][at][...] = one_hot(iota((lines, n_t * height), 0) == key)

    def build_gather(stage):
        lo, hi = plan.out_stages[stage]
        height = hi - lo
        spot = iota((n_t * height, 1), 0)
        for at, half in enumerate(plan.needs[stage]):
            here = (code == first + lo + lax.rem(spot, height)) & (rank == half)
            key = jnp.sum(jnp.where(here, line, 0), axis=1, keepdims=True)
            key = jnp.where(key > 0, key - 1 + lax.div(spot, height), -1)
            outs[stage]["gather"][at][...] = one_hot(iota((n_t * height, lines), 1) == key)

    def build_place():
        for stage, (lo, hi) in enumerate(plan.out_stages):
            height = hi - lo
            lane = iota((1, n_t * height), 1)
            lane = lax.div(lane, height) * width + lo + lax.rem(lane, height)
            outs[stage]["place"][...] = one_hot(code_col == lane)

    def build_mix():
        side = mix_mat.shape[0]
        pick = one_hot(lax.rem(iota((side, order), 0), order) == iota((side, order), 1))
        contract = (((1,), (1,)), ((), ()))
        tall = lax.dot_general(pick, a_ref[...], contract, preferred_element_type=jnp.float32)
        wide = lax.dot_general(
            tall.astype(BF16), pick, contract, preferred_element_type=jnp.float32
        )
        same = lax.div(iota((side, side), 0), order) == lax.div(iota((side, side), 1), order)
        mix_mat[...] = jnp.where(same, wide, 0.0).astype(BF16)

    def spread(half):
        mid = mids[plan.ranks.index(half)]

        def step(chunk, carry):
            for stage in plan.sources[half]:
                if half == plan.ranks[0] or stage not in plan.sources[plan.ranks[0]]:
                    arrived(ins[stage]["dst"], chunk, ins[stage]["recv"])
            mid["in_src"][chunk] = total(
                dot(mid["spread"][at][...], ins[stage]["dst"][chunk])
                for at, stage in enumerate(plan.sources[half])
            ).astype(BF16)
            send_d(mid["in_src"], mid["in_dst"], chunk, mid["in_send"], mid["in_recv"])
            return carry

        lax.fori_loop(0, in_chunks, step, 0)

    def mix(half):
        mid = mids[plan.ranks.index(half)]
        side = mix_mat.shape[0]

        def step(chunk, carry):
            arrived(mid["in_dst"], chunk, mid["in_recv"])
            for at in range(0, lines, side):
                mid["mixed"][at : at + side, in_columns(chunk)] = dot(
                    mix_mat[...], mid["in_dst"][chunk, at : at + side, :]
                ).astype(BF16)
            return carry

        lax.fori_loop(0, in_chunks, step, 0)

    def start_out(half, chunk):
        mid = mids[plan.ranks.index(half)]
        mid["out_src"][chunk] = dot(mid["mixed"][...], b_ref[:, out_columns(chunk)]).astype(BF16)
        send_d(mid["out_src"], mid["out_dst"], chunk, mid["out_send"], mid["out_recv"])

    def relay(stage, start, stop):
        lo, hi = plan.out_stages[stage]
        half = plan.needs[stage][-1]
        mid = mids[plan.ranks.index(half)]

        def step(chunk, carry):
            arrived(mid["out_dst"], chunk, mid["out_recv"])
            outs[stage]["src"][chunk] = total(
                dot(
                    outs[stage]["gather"][at][...],
                    mids[plan.ranks.index(need)]["out_dst"][chunk],
                )
                for at, need in enumerate(plan.needs[stage])
            ).astype(BF16)
            send_z(outs[stage], chunk, hi - lo)

            @pl.when(chunk + 2 < out_chunks)
            def _():
                start_out(half, chunk + 2)

            return carry

        lax.fori_loop(start, stop, step, 0)

    head = plan.ranks[0]
    build_spread(head)
    build_mix()
    build_gather(0)
    spread(head)
    mix(head)
    start_out(head, 0)
    start_out(head, 1)
    if plan.rest:
        build_place()
        relay(0, 0, out_chunks)
    else:
        build_spread(1)
        relay(0, 0, 1)
        spread(1)
        relay(0, 1, 3)
        mix(1)
        build_gather(1)
        relay(0, 3, out_chunks - 1)
        start_out(1, 0)
        relay(0, out_chunks - 1, out_chunks)
        start_out(1, 1)
        build_place()
        relay(1, 0, out_chunks)

    def place_chunk(chunk, carry):
        for part in outs:
            arrived(part["dst"], chunk, part["recv"])
        out_ref[:, out_columns(chunk)] = total(
            dot(part["place"][...], part["dst"][chunk]) for part in outs
        ).astype(BF16)
        return carry

    lax.fori_loop(0, out_chunks, place_chunk, 0)

    if flag is not None:
        pltpu.make_async_copy(flag["dst"], flag["dst"], flag["recv"]).wait()
        over_ref[...] = jnp.max(flag["dst"][...], axis=0, keepdims=True).astype(I32)
        part = flag["dst"].at[pl.ds(0, (n_dp - 1) * flag["src"].shape[0])]
        pltpu.make_async_copy(part, part, flag["send"]).wait()
    for stage, (lo, hi) in enumerate(plan.in_stages):
        sent(ins[stage]["src"], hi - lo, ins[stage]["send"])
    for mid in mids:
        sent(mid["in_src"], order, mid["in_send"])
        sent(mid["out_src"], order, mid["out_send"])
    for stage, (lo, hi) in enumerate(plan.out_stages):
        sent(outs[stage]["src"], hi - lo, outs[stage]["send"])


def exchange(rest, ids, slot, counts, rows_in, small, large):
    n_dp = lax.axis_size("dp")
    n_t = lax.axis_size("tensor")
    plan = Plan(n_dp, rest)
    rows, in_width = rows_in.shape
    order = small.shape[0]
    out_width = large.shape[1]
    lines = n_dp * order
    side = min(SIDE, lines)
    in_chunks = max(1, in_width // IN_CHUNK)
    in_cols = in_width // in_chunks
    out_chunks = max(4, out_width // OUT_CHUNK)
    out_cols = out_width // out_chunks

    def sems(n):
        return pltpu.SemaphoreType.DMA((n,))

    def buffer(*shape):
        return pltpu.VMEM(shape, BF16)

    def in_scratch(lo, hi):
        tall = n_t * (hi - lo)
        return {
            "pack": buffer(tall, rows),
            "src": buffer(in_chunks, tall, in_cols),
            "dst": buffer(in_chunks, tall, in_cols),
            "send": sems(in_chunks),
            "recv": sems(in_chunks),
        }

    def mid_scratch(half):
        heights = [plan.in_stages[s][1] - plan.in_stages[s][0] for s in plan.sources[half]]
        return {
            "spread": [buffer(lines, n_t * height) for height in heights],
            "in_src": buffer(in_chunks, lines, in_cols),
            "in_dst": buffer(in_chunks, lines, in_cols),
            "mixed": buffer(lines, in_width),
            "out_src": buffer(out_chunks, lines, out_cols),
            "out_dst": buffer(out_chunks, lines, out_cols),
            "in_send": sems(in_chunks),
            "in_recv": sems(in_chunks),
            "out_send": sems(out_chunks),
            "out_recv": sems(out_chunks),
        }

    def out_scratch(stage):
        lo, hi = plan.out_stages[stage]
        tall = n_t * (hi - lo)
        return {
            "gather": [buffer(tall, lines) for _ in plan.needs[stage]],
            "place": buffer(rows, tall),
            "src": buffer(out_chunks, tall, out_cols),
            "dst": buffer(out_chunks, tall, out_cols),
            "send": sems(out_chunks),
            "recv": sems(out_chunks),
        }

    scratch = [
        buffer(side, side),
        [in_scratch(lo, hi) for lo, hi in plan.in_stages],
        [mid_scratch(half) for half in plan.ranks],
        [out_scratch(stage) for stage in range(len(plan.out_stages))],
    ]
    out_shape = [jax.ShapeDtypeStruct((rows, out_width), BF16)]
    if not rest:
        out_shape.append(jax.ShapeDtypeStruct((1, 128), I32))
        scratch.append(
            {
                "src": pltpu.VMEM((8, 128), jnp.float32),
                "dst": pltpu.VMEM((8 * n_dp, 128), jnp.float32),
                "send": pltpu.SemaphoreType.DMA,
                "recv": pltpu.SemaphoreType.DMA,
            }
        )
    return pl.pallas_call(
        functools.partial(exchange_kernel, n_dp, n_t, plan),
        out_shape=out_shape,
        in_specs=[pl.BlockSpec(memory_space=pltpu.VMEM)] * 6,
        out_specs=[pl.BlockSpec(memory_space=pltpu.VMEM)] * len(out_shape),
        scratch_shapes=scratch,
        compiler_params=pltpu.CompilerParams(
            collective_id=1 if rest else 0,
            has_side_effects=True,
            vmem_limit_bytes=56 * 1024 * 1024,
        ),
        cost_estimate=pl.CostEstimate(
            flops=2 * RANKS * lines * in_width * out_width,
            bytes_accessed=10_000_000,
            transcendentals=0,
        ),
    )(ids, slot, counts, rows_in, small, large)


def on_device(rows_in, adapter_ids, row_counts, adapter_slot, adapter_a, adapter_b):
    args = (
        adapter_ids[None, :],
        adapter_slot[None, :],
        row_counts[None, :],
        rows_in,
        adapter_a[0],
        adapter_b[0],
    )
    done, over = exchange(False, *args)
    return lax.cond(
        over[0, 0] > 0,
        lambda done, *args: done + exchange(True, *args)[0],
        lambda done, *args: done,
        done,
        *args,
    )


def solution(mesh):
    return jax.shard_map(
        on_device,
        mesh=mesh,
        in_specs=(
            P("dp", "tensor"),
            P("dp"),
            P("dp"),
            P(),
            P(("dp", "tensor"), None, None),
            P(("dp", "tensor"), None, None),
        ),
        out_specs=P("dp", "tensor"),
        check_vma=False,
    )
```

```python
import functools

import jax
import jax.numpy as jnp
from jax import lax
from jax.experimental import pallas as pl
from jax.experimental.pallas import tpu as pltpu
from jax.sharding import PartitionSpec as P

RANKS = 2
IN_CHUNK = 128
OUT_CHUNK = 256
SIDE = 256
MESH = pl.DeviceIdType.MESH
BF16 = jnp.bfloat16
I32 = jnp.int32


def one_hot(mask):
    return jnp.where(mask, 1.0, 0.0).astype(BF16)


def dot(left, right):
    return jnp.dot(left, right, preferred_element_type=jnp.float32)


def iota(shape, axis):
    return lax.broadcasted_iota(I32, shape, axis)


def total(parts):
    return functools.reduce(lambda a, b: a + b, parts)


class Plan:
    def __init__(self, n_dp, rest):
        full = n_dp * RANKS
        self.tight = full * 3 // 4
        self.rest = rest
        if rest:
            self.width = full - self.tight
            self.units = ((0, self.width, 1, IN_CHUNK),)
        else:
            self.width = self.tight
            split = self.width - n_dp
            self.units = ((0, split, 1, IN_CHUNK), (split, self.width, 2, 2 * IN_CHUNK))


def exchange_kernel(n_dp, n_t, plan, ids_ref, slot_ref, count_ref, x_ref, a_ref, b_ref, *refs):
    if plan.rest:
        out_ref, units = refs
        flag = None
    else:
        out_ref, over_ref, units, flag = refs
    g = lax.axis_index("dp")
    t = lax.axis_index("tensor")
    rows = x_ref.shape[0]
    order = a_ref.shape[0]
    width = plan.width
    out_chunks, _, out_cols = units[0]["back_z"]["src"].shape

    barrier = pltpu.get_barrier_semaphore()

    def greet_t(step, carry):
        pl.semaphore_signal(
            barrier, inc=1, device_id=(g, lax.rem(t + step, n_t)), device_id_type=MESH
        )
        return carry

    def greet_d(step, carry):
        pl.semaphore_signal(
            barrier, inc=1, device_id=(lax.rem(g + step, n_dp), t), device_id_type=MESH
        )
        return carry

    lax.fori_loop(1, n_t, greet_t, 0)
    lax.fori_loop(1, n_dp, greet_d, 0)

    def send_z(part, chunk, height):
        src, dst, send_sem, recv_sem = part["src"], part["dst"], part["send"], part["recv"]

        def step(at, carry):
            half = (at + 1) // 2
            distance = n_t // 2 + jnp.where(at % 2 == 1, half, -half)
            peer = lax.rem(t + distance, n_t)
            pltpu.make_async_remote_copy(
                src_ref=src.at[chunk, pl.ds(pl.multiple_of(peer * height, height), height)],
                dst_ref=dst.at[chunk, pl.ds(pl.multiple_of(t * height, height), height)],
                send_sem=send_sem.at[chunk],
                recv_sem=recv_sem.at[chunk],
                device_id=(g, peer),
                device_id_type=MESH,
            ).start()
            return carry

        lax.fori_loop(0, n_t - 1, step, 0)
        own = pl.ds(pl.multiple_of(t * height, height), height)
        pltpu.make_async_copy(
            src.at[chunk, own], dst.at[chunk, own], recv_sem.at[chunk]
        ).start()

    def send_d(part, chunk, height):
        src, dst, send_sem, recv_sem = part["src"], part["dst"], part["send"], part["recv"]

        def step(at, carry):
            peer = lax.rem(g + at, n_dp)
            pltpu.make_async_remote_copy(
                src_ref=src.at[chunk, pl.ds(pl.multiple_of(peer * height, height), height)],
                dst_ref=dst.at[chunk, pl.ds(pl.multiple_of(g * height, height), height)],
                send_sem=send_sem.at[chunk],
                recv_sem=recv_sem.at[chunk],
                device_id=(peer, t),
                device_id_type=MESH,
            ).start()
            return carry

        lax.fori_loop(1, n_dp, step, 0)
        own = pl.ds(pl.multiple_of(g * height, height), height)
        pltpu.make_async_copy(
            src.at[chunk, own], dst.at[chunk, own], recv_sem.at[chunk]
        ).start()

    def arrived(part, chunk):
        dst = part["dst"].at[chunk]
        pltpu.make_async_copy(dst, dst, part["recv"].at[chunk]).wait()

    def sent(part, height):
        chunks, tall, _ = part["src"].shape

        def step(chunk, carry):
            most = part["src"].at[chunk, pl.ds(0, tall - height)]
            pltpu.make_async_copy(most, most, part["send"].at[chunk]).wait()
            return carry

        lax.fori_loop(0, chunks, step, 0)

    def columns_of(chunk, size):
        return pl.ds(pl.multiple_of(chunk * size, size), size)

    down = iota((rows, rows), 0)
    across = iota((rows, rows), 1)
    diagonal = down == across
    before = down < across

    def to_column(row):
        return jnp.sum(jnp.where(diagonal, row, 0), axis=1, keepdims=True)

    def to_row(column):
        return jnp.sum(jnp.where(diagonal, column, 0), axis=0, keepdims=True)

    def count(mask):
        return jnp.sum(jnp.where(mask, 1, 0), axis=0, keepdims=True)

    ids = ids_ref[...]
    ids_col = to_column(ids)
    owner_col = jnp.sum(jnp.where(ids_col == across, slot_ref[...], 0), axis=1, keepdims=True)
    rank = count((ids_col == ids) & before)
    owner = to_row(owner_col)
    column = lax.rem(owner, n_t)
    team = column * RANKS + rank
    team_col = to_column(team)
    live = iota((1, rows), 1) < count_ref[...]
    earlier = count((team_col == team) & before)
    firsts = count((team_col == column * RANKS) & (down < count_ref[...]))
    top = plan.tight - 1 - earlier
    over = live & (rank == 1) & (top < firsts)
    if plan.rest:
        code = jnp.where(over, column * width + firsts - 1 - top, -1)
    else:
        place = jnp.where(rank == 1, top, earlier)
        code = jnp.where(live & ~over, column * width + place, -1)

    def pack(unit, chunk):
        part = unit["go_z"]["src"]
        part[chunk] = dot(unit["pack"][...], x_ref[:, columns_of(chunk, part.shape[2])]).astype(BF16)

    for at, (lo, hi, _, _) in enumerate(plan.units):
        unit = units[at]
        height = hi - lo
        chunks = unit["go_z"]["src"].shape[0]
        spot = iota((n_t * height, 1), 0)
        spot = lax.div(spot, height) * width + lo + lax.rem(spot, height)
        unit["pack"][...] = one_hot(spot == code)
        pack(unit, 0)
        if at == 0:
            pl.semaphore_wait(barrier, n_dp + n_t - 2)

        def start_in(chunk, carry, unit=unit, height=height, chunks=chunks):
            send_z(unit["go_z"], chunk, height)

            @pl.when(chunk < chunks - 1)
            def _():
                pack(unit, chunk + 1)

            return carry

        lax.fori_loop(0, chunks, start_in, 0)

    if flag is not None:
        tile = flag["src"].shape[0]
        most = jnp.max(jnp.where(over, 1.0, 0.0), axis=1, keepdims=True)
        flag["src"][...] = jnp.broadcast_to(most, flag["src"].shape)
        spot = pl.ds(pl.multiple_of(g * tile, tile), tile)

        def tell(step, carry):
            pltpu.make_async_remote_copy(
                src_ref=flag["src"],
                dst_ref=flag["dst"].at[spot],
                send_sem=flag["send"],
                recv_sem=flag["recv"],
                device_id=(lax.rem(g + step, n_dp), t),
                device_id_type=MESH,
            ).start()
            return carry

        lax.fori_loop(1, n_dp, tell, 0)
        pltpu.make_async_copy(flag["src"], flag["dst"].at[spot], flag["recv"]).start()

    code_col = to_column(code)
    rank_col = lax.rem(team_col, RANKS)
    team_row, team_column = lax.div(owner, n_t) * order, lax.div(owner_col, n_t) * order
    first = t * width

    def build_spread(at):
        lo, hi, copies, _ = plan.units[at]
        height = hi - lo
        mat = units[at]["spread"]
        line = team_column * copies + 1 + (rank_col if copies > 1 else 0)
        lane = iota((1, n_t * height), 1)
        here = code_col == first + lo + lax.rem(lane, height)
        key = jnp.sum(jnp.where(here, line, 0), axis=0, keepdims=True)
        key = jnp.where(key > 0, key - 1 + lax.div(lane, height) * copies, -1)
        mat[...] = one_hot(iota(mat.shape, 0) == key)

    def build_gather(at):
        lo, hi, copies, _ = plan.units[at]
        height = hi - lo
        mat = units[at]["gather"]
        line = team_row * copies + 1 + (rank if copies > 1 else 0)
        spot = iota((n_t * height, 1), 0)
        here = code == first + lo + lax.rem(spot, height)
        key = jnp.sum(jnp.where(here, line, 0), axis=1, keepdims=True)
        key = jnp.where(key > 0, key - 1 + lax.div(spot, height) * copies, -1)
        mat[...] = one_hot(iota(mat.shape, 1) == key)

    def build_place(at):
        lo, hi, _, _ = plan.units[at]
        height = hi - lo
        lane = iota((1, n_t * height), 1)
        lane = lax.div(lane, height) * width + lo + lax.rem(lane, height)
        units[at]["place"][...] = one_hot(code_col == lane)

    def build_mix(at):
        copies = plan.units[at][2]
        mat = units[at]["mix"]
        side = mat.shape[0]
        unit_of = lax.rem(lax.div(iota((side, order), 0), copies), order)
        pick = one_hot(unit_of == iota((side, order), 1))
        contract = (((1,), (1,)), ((), ()))
        tall = lax.dot_general(pick, a_ref[...], contract, preferred_element_type=jnp.float32)
        wide = lax.dot_general(
            tall.astype(BF16), pick, contract, preferred_element_type=jnp.float32
        )
        one, two = iota((side, side), 0), iota((side, side), 1)
        same = (lax.div(one, order * copies) == lax.div(two, order * copies)) & (
            lax.rem(one, copies) == lax.rem(two, copies)
        )
        mat[...] = jnp.where(same, wide, 0.0).astype(BF16)

    def spread(at):
        unit = units[at]
        copies = plan.units[at][2]

        def step(chunk, carry):
            arrived(unit["go_z"], chunk)
            unit["go_d"]["src"][chunk] = dot(
                unit["spread"][...], unit["go_z"]["dst"][chunk]
            ).astype(BF16)
            send_d(unit["go_d"], chunk, order * copies)
            return carry

        lax.fori_loop(0, unit["go_z"]["src"].shape[0], step, 0)

    def mix(at):
        unit = units[at]
        side = unit["mix"].shape[0]
        chunks, lines, cols = unit["go_d"]["dst"].shape

        def step(chunk, carry):
            arrived(unit["go_d"], chunk)
            for low in range(0, lines, side):
                unit["mixed"][low : low + side, columns_of(chunk, cols)] = dot(
                    unit["mix"][...], unit["go_d"]["dst"][chunk, low : low + side, :]
                ).astype(BF16)
            return carry

        lax.fori_loop(0, chunks, step, 0)

    def start_out(at, chunk):
        unit = units[at]
        unit["back_d"]["src"][chunk] = dot(
            unit["mixed"][...], b_ref[:, columns_of(chunk, out_cols)]
        ).astype(BF16)
        send_d(unit["back_d"], chunk, order * plan.units[at][2])

    def relay(at, start, stop):
        unit = units[at]
        lo, hi, _, _ = plan.units[at]

        def step(chunk, carry):
            arrived(unit["back_d"], chunk)
            unit["back_z"]["src"][chunk] = dot(
                unit["gather"][...], unit["back_d"]["dst"][chunk]
            ).astype(BF16)
            send_z(unit["back_z"], chunk, hi - lo)

            @pl.when(chunk + 2 < out_chunks)
            def _():
                start_out(at, chunk + 2)

            return carry

        lax.fori_loop(start, stop, step, 0)

    build_spread(0)
    build_mix(0)
    build_gather(0)
    spread(0)
    mix(0)
    start_out(0, 0)
    start_out(0, 1)
    if plan.rest:
        build_place(0)
        relay(0, 0, out_chunks)
    else:
        build_spread(1)
        relay(0, 0, 2)
        build_mix(1)
        spread(1)
        relay(0, 2, 4)
        build_gather(1)
        mix(1)
        start_out(1, 0)
        relay(0, 4, out_chunks - 1)
        start_out(1, 1)
        relay(0, out_chunks - 1, out_chunks)
        relay(1, 0, out_chunks)
        build_place(0)
        build_place(1)

    def place_chunk(chunk, carry):
        for unit in units:
            arrived(unit["back_z"], chunk)
        out_ref[:, columns_of(chunk, out_cols)] = total(
            dot(unit["place"][...], unit["back_z"]["dst"][chunk]) for unit in units
        ).astype(BF16)
        return carry

    lax.fori_loop(0, out_chunks, place_chunk, 0)

    if flag is not None:
        pltpu.make_async_copy(flag["dst"], flag["dst"], flag["recv"]).wait()
        over_ref[...] = jnp.max(flag["dst"][...], axis=0, keepdims=True).astype(I32)
        part = flag["dst"].at[pl.ds(0, (n_dp - 1) * flag["src"].shape[0])]
        pltpu.make_async_copy(part, part, flag["send"]).wait()
    for unit, (lo, hi, copies, _) in zip(units, plan.units):
        sent(unit["go_z"], hi - lo)
        sent(unit["go_d"], order * copies)
        sent(unit["back_d"], order * copies)
        sent(unit["back_z"], hi - lo)


def exchange(rest, ids, slot, counts, rows_in, small, large):
    n_dp = lax.axis_size("dp")
    n_t = lax.axis_size("tensor")
    plan = Plan(n_dp, rest)
    rows, in_width = rows_in.shape
    order = small.shape[0]
    out_width = large.shape[1]
    out_chunks = max(4, out_width // OUT_CHUNK)

    def buffer(*shape):
        return pltpu.VMEM(shape, BF16)

    def copied(chunks, tall, cols):
        return {
            "src": buffer(chunks, tall, cols),
            "dst": buffer(chunks, tall, cols),
            "send": pltpu.SemaphoreType.DMA((chunks,)),
            "recv": pltpu.SemaphoreType.DMA((chunks,)),
        }

    def unit_scratch(lo, hi, copies, cols):
        tall = n_t * (hi - lo)
        lines = n_dp * order * copies
        side = min(SIDE, lines)
        in_chunks = max(1, in_width // cols)
        return {
            "pack": buffer(tall, rows),
            "spread": buffer(lines, tall),
            "gather": buffer(tall, lines),
            "place": buffer(rows, tall),
            "mix": buffer(side, side),
            "mixed": buffer(lines, in_width),
            "go_z": copied(in_chunks, tall, in_width // in_chunks),
            "go_d": copied(in_chunks, lines, in_width // in_chunks),
            "back_d": copied(out_chunks, lines, out_width // out_chunks),
            "back_z": copied(out_chunks, tall, out_width // out_chunks),
        }

    scratch = [[unit_scratch(*unit) for unit in plan.units]]
    out_shape = [jax.ShapeDtypeStruct((rows, out_width), BF16)]
    if not rest:
        out_shape.append(jax.ShapeDtypeStruct((1, 128), I32))
        scratch.append(
            {
                "src": pltpu.VMEM((8, 128), jnp.float32),
                "dst": pltpu.VMEM((8 * n_dp, 128), jnp.float32),
                "send": pltpu.SemaphoreType.DMA,
                "recv": pltpu.SemaphoreType.DMA,
            }
        )
    return pl.pallas_call(
        functools.partial(exchange_kernel, n_dp, n_t, plan),
        out_shape=out_shape,
        in_specs=[pl.BlockSpec(memory_space=pltpu.VMEM)] * 6,
        out_specs=[pl.BlockSpec(memory_space=pltpu.VMEM)] * len(out_shape),
        scratch_shapes=scratch,
        compiler_params=pltpu.CompilerParams(
            collective_id=1 if rest else 0,
            has_side_effects=True,
            vmem_limit_bytes=56 * 1024 * 1024,
        ),
        cost_estimate=pl.CostEstimate(
            flops=2 * RANKS * n_dp * order * in_width * out_width,
            bytes_accessed=10_000_000,
            transcendentals=0,
        ),
    )(ids, slot, counts, rows_in, small, large)


def on_device(rows_in, adapter_ids, row_counts, adapter_slot, adapter_a, adapter_b):
    args = (
        adapter_ids[None, :],
        adapter_slot[None, :],
        row_counts[None, :],
        rows_in,
        adapter_a[0],
        adapter_b[0],
    )
    done, over = exchange(False, *args)
    return lax.cond(
        over[0, 0] > 0,
        lambda done, *args: done + exchange(True, *args)[0],
        lambda done, *args: done,
        done,
        *args,
    )


def solution(mesh):
    return jax.shard_map(
        on_device,
        mesh=mesh,
        in_specs=(
            P("dp", "tensor"),
            P("dp"),
            P("dp"),
            P(),
            P(("dp", "tensor"), None, None),
            P(("dp", "tensor"), None, None),
        ),
        out_specs=P("dp", "tensor"),
        check_vma=False,
    )
```
